256 devices in a mesh: seq: 32 (over y, x, core), head: 8 (over z).
Axes of the slice: x: 4, y: 4, z: 8, core: 2. Of those that a mesh axis runs over, the one named last changes fastest.
Arguments:
- query_rows: bfloat16 [32768, 4096], P(('seq', 'head')), may hold values from -6 to 6
- key_rows: bfloat16 [32768, 4096], P(('seq', 'head')), may hold values from -6 to 6
- value_rows: bfloat16 [32768, 4096], P(('seq', 'head')), may hold values from -6 to 6
- log_decay: bfloat16 [32768, 4096], P(('seq', 'head')), may hold values from -1 to 0
- write_rate: bfloat16 [32768, 32], P(('seq', 'head')), may hold values from 0.0039 to 0.91
Outputs:
- attended: bfloat16 [32768, 4096], P(('seq', 'head'))
The draws below stay inside these ranges and needn't reach their ends.
All inputs are finite; a program needn't handle non-finite values.
Results may differ from the reference program's by a relative error of at most 0.0012.
Values may be sent and summed in bfloat16 or wider, within the bound.
A program may use at most 192 MiB of HBM per device.

```python
import math
import jax
import jax.numpy as jnp
from jax import lax

HEADS = 32
DK = 128
BLOCK = 64
TOK_DEV = 128
TOKENS = 32768


def log_between(key, shape, lower, upper):
    return jnp.exp(jax.random.uniform(key, shape, jnp.float32, math.log(lower), math.log(upper)))


def draw_key_rows(key, part):
    key = jax.random.fold_in(key, 3)
    streams = jax.random.split(key, 2)
    common = 1.5 * jax.random.normal(streams[0], (1, HEADS * DK), jnp.float32)
    noise = jax.random.normal(streams[1], (TOKENS, HEADS * DK), jnp.float32)
    return jnp.clip(common + noise, -6.0, 6.0).astype(jnp.bfloat16)


def draw_log_decay(key, part):
    channel_share = 0.5
    key = jax.random.fold_in(key, 1)
    streams = jax.random.split(key, 7)
    slow_chan = jax.random.uniform(streams[0], (HEADS, DK)) < channel_share
    fast_rate = log_between(streams[1], (HEADS, DK), 1.0 / 400.0, 1.0 / 30.0)
    slow_rate = log_between(streams[2], (HEADS, DK), 0.1, 0.4) / TOKENS
    base = jnp.where(slow_chan, slow_rate, fast_rate).reshape(1, 1, HEADS * DK)
    groups = TOKENS // TOK_DEV
    group_factor = log_between(streams[3], (groups, 1, HEADS * DK), 0.5, 2.0)
    token_factor = log_between(streams[4], (groups, TOK_DEV, HEADS * DK), 0.5, 2.0)
    rate = (base * group_factor * token_factor).reshape(TOKENS, HEADS * DK)
    spots = jax.random.randint(streams[5], (2,), 0, TOKENS)
    struck = jnp.any(jnp.arange(TOKENS)[:, None] == spots[None, :], axis=1, keepdims=True)
    losses = jnp.log(jax.random.uniform(streams[6], (1, HEADS * DK), jnp.float32, 0.5, 0.8))
    return (jnp.where(struck, losses, 0.0) - rate).astype(jnp.bfloat16)


def draw_write_rate(key, part):
    share = 0.5
    key = jax.random.fold_in(key, 2)
    streams = jax.random.split(key, 3)
    heads_slow = jax.random.uniform(streams[2], (HEADS,)) < share
    fast_rate = jax.random.uniform(streams[0], (TOKENS, HEADS), jnp.float32, 0.2, 0.9)
    slow_rate = log_between(streams[1], (TOKENS, HEADS), 0.004, 0.0095)
    return jnp.where(heads_slow[None, :], slow_rate, fast_rate).astype(jnp.bfloat16)


def levels(own_key, shape, cuts, low, top_value):
    def one(axis_at, blocks):
        heights = jax.random.uniform(jax.random.fold_in(jax.random.fold_in(own_key, 6), axis_at), (blocks,), jnp.float32, low / len(cuts), top_value / len(cuts))
        return jnp.repeat(jnp.exp(heights), shape[axis_at] // blocks).reshape((-1,) + (1,) * (len(shape) - axis_at - 1))

    gain = one(*cuts[0])
    for cut in cuts[1:]:
        gain = gain * one(*cut)
    return gain


def normal_values(own_key, extent, scale, most, cuts=(), kind=jnp.bfloat16):
    values = jax.random.normal(own_key, extent, jnp.float32) * scale
    if len(cuts) > 0:
        values = levels(own_key, extent, cuts, -0.22, 0.18) * values
    return jnp.clip(values, min=-most, max=most).astype(kind)


def setup_inputs(seed: int = 0) -> dict:
    splits = jax.random.split(jax.random.key(seed), 6)
    return {
        "query_rows": normal_values(splits[0], (TOKENS, HEADS * DK), 1.0, 6.0, ((0, 256),)),
        "key_rows": draw_key_rows(jax.random.fold_in(splits[5], 71), 0),
        "value_rows": normal_values(splits[2], (TOKENS, HEADS * DK), 1.0, 6.0, ((0, 256),)),
        "log_decay": draw_log_decay(jax.random.fold_in(splits[5], 71), 0),
        "write_rate": draw_write_rate(jax.random.fold_in(splits[5], 71), 0),
    }


epsilon = 1e-06
highest = lax.Precision.HIGHEST

def unit_rows(matrix):
    return matrix * lax.rsqrt(lax.optimization_barrier(jnp.sum(matrix * matrix, axis=-1, keepdims=True)) + epsilon)

def block_maps(query_blk, key_blk, value_blk, decay_blk, rate_blk):
    length = query_blk.shape[2]
    width = query_blk.shape[3]
    query_unit = unit_rows(query_blk)
    key_unit = unit_rows(key_blk)
    cumulative = jnp.cumsum(decay_blk, axis=2)
    middle = cumulative[:, :, length // 2:length // 2 + 1, :]
    closing = cumulative[:, :, length - 1:length, :]
    ahead = key_unit * jnp.exp(cumulative - middle)
    behind = key_unit * jnp.exp(middle - cumulative)
    query_ahead = query_unit * jnp.exp(cumulative - middle)
    positions = jnp.arange(length)
    strict = positions[:, None] > positions[None, :]
    inclusive = positions[:, None] >= positions[None, :]
    weights = rate_blk[:, :, None, :]
    among = jnp.where(strict, jnp.einsum('nhid,nhjd->nhij', ahead, behind, precision=highest), 0.0) * weights
    attend = jnp.where(inclusive, jnp.einsum('nhid,nhjd->nhij', query_ahead, behind, precision=highest), 0.0) * weights
    system = jnp.eye(length, dtype=jnp.float32) + among
    key_past = key_unit * jnp.exp(cumulative)
    solved = jax.scipy.linalg.solve_triangular(system, jnp.concatenate([value_blk, key_past], axis=-1), lower=True, unit_diagonal=True)
    update = solved[..., :width]
    reach = solved[..., width:]
    written = key_unit * jnp.exp(closing - cumulative) * rate_blk[..., None]
    decay_diag = jnp.eye(width, dtype=jnp.float32) * jnp.exp(closing)[:, :, 0, :, None]
    transition = decay_diag - jnp.einsum('nhjd,nhje->nhde', written, reach, precision=highest)
    carried = jnp.einsum('nhjd,nhje->nhde', written, update, precision=highest)
    readout = query_unit * jnp.exp(cumulative) - jnp.einsum('nhij,nhjd->nhid', attend, reach, precision=highest)
    local_part = jnp.einsum('nhij,nhjd->nhid', attend, update, precision=highest)
    return (readout, local_part, transition, carried)

def reference(query_rows, key_rows, value_rows, log_decay, write_rate):
    total = TOKENS // BLOCK
    width = HEADS * DK

    def shaped(matrix):
        return matrix.reshape(total, BLOCK, width)

    def advance(memory, pieces):
        blocks = [piece.reshape(1, BLOCK, HEADS, DK).transpose(0, 2, 1, 3).astype(jnp.float32) for piece in pieces[:4]]
        rates = pieces[4].reshape(1, BLOCK, HEADS).transpose(0, 2, 1).astype(jnp.float32)
        readout, local_part, transition, carried = block_maps(blocks[0], blocks[1], blocks[2], blocks[3], rates)
        result = local_part[0] + jnp.einsum('hid,hde->hie', readout[0], memory, precision=highest)
        memory = jnp.einsum('hde,hef->hdf', transition[0], memory, precision=highest) + carried[0]
        return (memory, result.transpose(1, 0, 2).reshape(BLOCK, width).astype(jnp.bfloat16))
    memory = jnp.zeros((HEADS, DK, DK), jnp.float32)
    pieces = (shaped(query_rows), shaped(key_rows), shaped(value_rows), shaped(log_decay), write_rate.reshape(total, BLOCK, HEADS))
    memory, outputs = lax.scan(advance, memory, pieces)
    return outputs.reshape(TOKENS, width)
```

```python
import functools

import jax
import jax.numpy as jnp
from jax import lax
from jax.experimental import pallas as pl
from jax.experimental.pallas import tpu as pltpu
from jax.sharding import PartitionSpec as P

DK = 128
L = 128
F32 = jnp.float32
BF = jnp.bfloat16
MESH = pl.DeviceIdType.MESH


def split(x):
    hi = x.astype(BF)
    return hi, (x - hi.astype(F32)).astype(BF)


def mm(a, b, dims=((1,), (0,))):
    return lax.dot_general(a, b, (dims, ((), ())), preferred_element_type=F32)


def dot3(a, b, turned=False):
    dims = ((1,), (1,)) if turned else ((1,), (0,))
    wide = jnp.concatenate([a[0], a[1]], 1)
    twice = jnp.concatenate([b[0], b[0]], 1 if turned else 0)
    return mm(wide, twice, dims) + mm(a[0], b[1], dims)


def dot2(a, b):
    return mm(jnp.concatenate([a[0], a[1]], 1), jnp.concatenate([b, b], 0))


def unit_rows(x):
    return x * lax.rsqrt(jnp.sum(x * x, axis=-1, keepdims=True) + 1e-6)


def block_maps(units):
    row = lax.broadcasted_iota(jnp.int32, (L, L), 0)
    col = lax.broadcasted_iota(jnp.int32, (L, L), 1)
    eye = row == col
    tri = (row >= col).astype(BF)
    pre = []
    for q, k, v, g, rate in units:
        cum = mm(tri, g)
        qn = unit_rows(q.astype(F32))
        kn = unit_rows(k.astype(F32))
        mid = cum[L // 2 : L // 2 + 1, :]
        closing = cum[L - 1 : L, :]
        up = jnp.exp(cum - mid)
        past = jnp.exp(cum)
        kr = kn * rate
        pre.append(
            (
                split(jnp.concatenate([kn * up, qn * up], 0)),
                split(kr * jnp.exp(mid - cum)),
                split(kn * past),
                jnp.concatenate([qn * past, jnp.where(eye, jnp.exp(closing), 0.0)], 0),
                (kr * jnp.exp(closing - cum)).T,
                v,
            )
        )
    pairs = [dot3(p[0], p[1], True) for p in pre]
    among = [jnp.where(row > col, m[:L], 0.0) for m in pairs]
    attend = [jnp.where(row >= col, m[L:], 0.0) for m in pairs]
    inverse = None
    size = 1
    while size < L:
        lower = jnp.logical_and(
            row // (2 * size) == col // (2 * size),
            jnp.logical_and((row // size) % 2 == 1, (col // size) % 2 == 0),
        )
        if inverse is None:
            inverse = [jnp.where(eye, 1.0, 0.0) - jnp.where(lower, a, 0.0) for a in among]
        else:
            halves = [split(x) for x in inverse]
            right = [
                split(dot3(split(jnp.where(lower, a, 0.0)), x)) for a, x in zip(among, halves)
            ]
            inverse = [x - dot3(h, r) for x, h, r in zip(inverse, halves, right)]
        size *= 2
    both = [
        split(dot3(split(jnp.concatenate([a, p[4]], 0)), split(x)))
        for a, p, x in zip(attend, pre, inverse)
    ]
    return [(p[3] - dot3(z, p[2]), dot2(z, p[5])) for z, p in zip(both, pre)]


def compose(later, earlier):
    product = dot3(split(later[:, :DK]), split(earlier))
    return jnp.concatenate([product[:, :DK], product[:, DK:] + later[:, DK:]], 1)


def advance(span, state):
    return dot3(split(span[:, :DK]), split(state)) + span[:, DK:]


def head_maps(q_ref, k_ref, v_ref, g_ref, rate_ref, ab_ref, tc_ref, group):
    blocks = q_ref.shape[0] // L
    prefix = None
    for first in range(0, blocks, group):
        rows = [pl.ds(b * L, L) for b in range(first, first + group)]
        maps = block_maps(
            [(q_ref[r, :], k_ref[r, :], v_ref[r, :], g_ref[r, :], rate_ref[r, :]) for r in rows]
        )
        for r, (moves, adds) in zip(rows, maps):
            if prefix is None:
                both = jnp.concatenate([moves, adds], 1)
            else:
                both = dot3(split(moves), split(prefix))
                both = jnp.concatenate([both[:, :DK], both[:, DK:] + adds], 1)
            ab_ref[r, :] = both[:L]
            prefix = both[L:]
    tc_ref[...] = prefix


def maps_kernel(q_ref, k_ref, v_ref, g_ref, rate_ref, ab_ref, tc_ref):
    head_maps(q_ref, k_ref, v_ref, g_ref, rate_ref.at[0], ab_ref.at[0], tc_ref.at[0], 8)


def scan_kernel(
    tc_ref, ab_ref, out_ref, sib, chip, xb, yb, enter, send_sem, recv_sem
):
    me = lax.axis_index("seq")
    z = lax.axis_index("head")
    core, x, y = me % 2, (me // 2) % 4, me // 8
    peer = me + 1 - 2 * core
    x_peers = [y * 8 + ((x + d) % 4) * 2 + core for d in (1, 2, 3)]
    y_peers = [((y + d) % 4) * 8 + x * 2 + core for d in (1, 2, 3)]
    barrier = pltpu.get_barrier_semaphore()
    for to in [peer] + x_peers + y_peers:
        pl.semaphore_signal(barrier, inc=1, device_id=(to, z), device_id_type=MESH)
    pl.semaphore_wait(barrier, 7)

    def copy(src, dst, j, n, to):
        return pltpu.make_async_remote_copy(
            src_ref=src,
            dst_ref=dst,
            send_sem=send_sem.at[j, n],
            recv_sem=recv_sem.at[j, n],
            device_id=(to, z),
            device_id_type=MESH,
        )

    live = []
    for j in range(2):
        c = copy(tc_ref.at[2 * j + 1 - core], sib.at[j], j, 0, peer)
        c.start()
        live.append(c)
    firsts = []
    for j in range(2):
        live[j].wait_recv()
        own, other = tc_ref[2 * j + core], sib[j]
        first = jnp.where(core == 0, own, other)
        chip[j] = compose(jnp.where(core == 0, other, own), first)
        firsts.append(first)
        for d in range(3):
            c = copy(chip.at[j], xb.at[j, d], j, 1 + d, x_peers[d])
            c.start()
            live.append(c)
    befores = []
    for j in range(2):
        for d in range(3):
            live[2 + 3 * j + d].wait_recv()
        spans = []
        for i in range(4):
            far = (x - i + 4) % 4
            spans.append(
                jnp.where(
                    far == 0,
                    chip[j],
                    jnp.where(far == 1, xb[j, 0], jnp.where(far == 2, xb[j, 1], xb[j, 2])),
                )
            )
        two = compose(spans[1], spans[0])
        three = compose(spans[2], two)
        total = compose(compose(spans[3], spans[2]), two)
        befores.append((spans[0], two, three))
        yb[j, 3] = total
        for d in range(3):
            c = copy(yb.at[j, 3], yb.at[j, d], j, 4 + d, y_peers[d])
            c.start()
            live.append(c)
    for j in range(2):
        for d in range(3):
            live[8 + 3 * j + d].wait_recv()
        spans = []
        for i in range(3):
            far = (y - i + 4) % 4
            spans.append(
                jnp.where(
                    far == 0,
                    yb[j, 3],
                    jnp.where(far == 1, yb[j, 0], jnp.where(far == 2, yb[j, 1], yb[j, 2])),
                )
            )
        one = spans[0][:, DK:]
        two = advance(spans[1], one)
        three = advance(spans[2], two)
        state = jnp.where(y == 0, 0.0, jnp.where(y == 1, one, jnp.where(y == 2, two, three)))
        before = jnp.where(
            x == 1, befores[j][0], jnp.where(x == 2, befores[j][1], befores[j][2])
        )
        state = jnp.where(x == 0, state, advance(before, state))
        after = advance(firsts[j], state)
        enter[j, 0] = jnp.where(core == 0, state, after)
        enter[j, 1] = jnp.where(core == 0, after, state)
        c = copy(enter.at[j, 1], enter.at[j, 2], j, 7, peer)
        c.start()
        live.append(c)
    for j in range(2):
        live[14 + j].wait_recv()
        for half in range(2):
            h = 2 * j + half
            state = jnp.where(core == half, enter[j, 0], enter[j, 2])
            ab = ab_ref[h]
            out = dot3(split(ab[:, :DK]), split(state)) + ab[:, DK:]
            out_ref[:, h * DK : (h + 1) * DK] = out.astype(BF)
    for c in live:
        c.wait_send()


def local(query_rows, key_rows, value_rows, log_decay, write_rate):
    def moved(a):
        return lax.all_to_all(a, "head", split_axis=1, concat_axis=0, tiled=True)

    rate = moved(write_rate).astype(F32).T[:, :, None]
    g, k, v, q = moved(log_decay), moved(key_rows), moved(value_rows), moved(query_rows)
    rows, heads = g.shape[0], g.shape[1] // DK
    cols = pl.BlockSpec((rows, DK), lambda h: (0, h))
    ab, tc = pl.pallas_call(
        maps_kernel,
        grid=(heads,),
        in_specs=[cols] * 4 + [pl.BlockSpec((1, rows, 1), lambda h: (h, 0, 0))],
        out_specs=[
            pl.BlockSpec((1, rows, 2 * DK), lambda h: (h, 0, 0)),
            pl.BlockSpec((1, DK, 2 * DK), lambda h: (h, 0, 0)),
        ],
        out_shape=[
            jax.ShapeDtypeStruct((heads, rows, 2 * DK), F32),
            jax.ShapeDtypeStruct((heads, DK, 2 * DK), F32),
        ],
        compiler_params=pltpu.CompilerParams(vmem_limit_bytes=48 * 2**20),
    )(q, k, v, g, rate)
    whole = pl.BlockSpec(memory_space=pltpu.VMEM)
    out = pl.pallas_call(
        scan_kernel,
        in_specs=[whole, whole],
        out_specs=whole,
        out_shape=jax.ShapeDtypeStruct((rows, heads * DK), BF),
        scratch_shapes=[
            pltpu.VMEM((2, DK, 2 * DK), F32),
            pltpu.VMEM((2, DK, 2 * DK), F32),
            pltpu.VMEM((2, 3, DK, 2 * DK), F32),
            pltpu.VMEM((2, 4, DK, 2 * DK), F32),
            pltpu.VMEM((2, 3, DK, DK), F32),
            pltpu.SemaphoreType.DMA((2, 8)),
            pltpu.SemaphoreType.DMA((2, 8)),
        ],
        compiler_params=pltpu.CompilerParams(
            vmem_limit_bytes=48 * 2**20, collective_id=0, has_side_effects=True
        ),
    )(tc, ab)
    return lax.all_to_all(out, "head", split_axis=0, concat_axis=1, tiled=True)


def solution(mesh):
    spec = P(("seq", "head"), None)
    return jax.shard_map(
        local, mesh=mesh, in_specs=(spec,) * 5, out_specs=spec, check_vma=False
    )
```

```python
import functools

import jax
import jax.numpy as jnp
from jax import lax
from jax.experimental import pallas as pl
from jax.experimental.pallas import tpu as pltpu
from jax.sharding import PartitionSpec as P

DK = 128
L = 128
RING = 8
HEADS = 4
GROUP = 4
F32 = jnp.float32
BF = jnp.bfloat16
MESH = pl.DeviceIdType.MESH


def split(x):
    hi = x.astype(BF)
    return hi, (x - hi.astype(F32)).astype(BF)


def mm(a, b, dims=((1,), (0,))):
    return lax.dot_general(a, b, (dims, ((), ())), preferred_element_type=F32)


def dot3(a, b, turned=False):
    dims = ((1,), (1,)) if turned else ((1,), (0,))
    wide = jnp.concatenate([a[0], a[1]], 1)
    twice = jnp.concatenate([b[0], b[0]], 1 if turned else 0)
    return mm(wide, twice, dims) + mm(a[0], b[1], dims)


def dot2(a, b):
    return mm(jnp.concatenate([a[0], a[1]], 1), jnp.concatenate([b, b], 0))


def unit_rows(x):
    return x * lax.rsqrt(jnp.sum(x * x, axis=-1, keepdims=True) + 1e-6)


def masks():
    row = lax.broadcasted_iota(jnp.int32, (L, L), 0)
    col = lax.broadcasted_iota(jnp.int32, (L, L), 1)
    return row, col


def unit_inverse(among):
    row, col = masks()
    eye = jnp.where(row == col, 1.0, 0.0)
    inverse = None
    size = 1
    while size < L:
        lower = jnp.logical_and(
            row // (2 * size) == col // (2 * size),
            jnp.logical_and((row // size) % 2 == 1, (col // size) % 2 == 0),
        )
        if inverse is None:
            inverse = [eye - jnp.where(lower, a, 0.0) for a in among]
        else:
            halves = [split(x) for x in inverse]
            right = [
                split(dot3(split(jnp.where(lower, a, 0.0)), x)) for a, x in zip(among, halves)
            ]
            inverse = [x - dot3(h, r) for x, h, r in zip(inverse, halves, right)]
        size *= 2
    return inverse


def running(g):
    row, col = masks()
    cum = mm((row >= col).astype(BF), g)
    return cum, cum[L // 2 : L // 2 + 1, :], cum[L - 1 : L, :]


def compose(later, earlier):
    product = dot3(split(later[:, :DK]), split(earlier))
    return jnp.concatenate([product[:, :DK], product[:, DK:] + later[:, DK:]], 1)


def advance(span, state):
    return dot3(split(span[:, :DK]), split(state)) + span[:, DK:]


def kernel(
    q_ref, k_ref, v_ref, g_ref, rate_ref, out_ref,
    kb, gb, vb, qb, rb, ob, inv, past, behind, spans,
    sib, chip, first, xb, before, yb, enter,
    in_send, in_recv, out_send, out_recv, rate_send, rate_recv, scan_send, scan_recv,
):
    me = lax.axis_index("seq")
    z = lax.axis_index("head")
    core, x, y = me % 2, (me // 2) % 4, me // 8
    peer = me + 1 - 2 * core
    x_peers = [y * 8 + ((x + d) % 4) * 2 + core for d in (1, 2, 3)]
    y_peers = [((y + d) % 4) * 8 + x * 2 + core for d in (1, 2, 3)]
    row, col = masks()
    eye = row == col

    barrier = pltpu.get_barrier_semaphore()

    def greet(d, carry):
        pl.semaphore_signal(barrier, inc=1, device_id=(me, (z + d) % RING), device_id_type=MESH)
        return carry

    lax.fori_loop(1, RING, greet, 0)
    for to in [peer] + x_peers + y_peers:
        pl.semaphore_signal(barrier, inc=1, device_id=(to, z), device_id_type=MESH)
    pl.semaphore_wait(barrier, RING + 6)

    def columns(owner, h):
        return pl.ds(pl.multiple_of((owner * HEADS + h) * DK, DK), DK)

    def remote(src, dst, send, recv, to):
        return pltpu.make_async_remote_copy(
            src_ref=src, dst_ref=dst, send_sem=send, recv_sem=recv, device_id=to, device_id_type=MESH
        )

    arrays = ((k_ref, kb), (g_ref, gb), (v_ref, vb), (q_ref, qb))

    def incoming(a, h, d):
        to = (z + d) % RING
        src, dst = arrays[a]
        return remote(
            src.at[:, columns(to, h)], dst.at[h, d], in_send.at[a, h, d], in_recv.at[a, h, d], (me, to)
        )

    def own_block(a, h):
        src, dst = arrays[a]
        return pltpu.make_async_copy(src.at[:, columns(z, h)], dst.at[h, 0], in_recv.at[a, h, 0])

    def rates(d):
        to = (z + d) % RING
        return remote(rate_ref, rb.at[d], rate_send.at[d], rate_recv.at[d], (me, to))

    def outgoing(h, d):
        to = (z + d) % RING
        return remote(
            ob.at[h, d], out_ref.at[:, columns(z, h)], out_send.at[h, d], out_recv.at[h, d], (me, to)
        )

    def own_out(h):
        return pltpu.make_async_copy(ob.at[h, 0], out_ref.at[:, columns(z, h)], out_recv.at[h, 0])

    own_rate = pltpu.make_async_copy(rate_ref, rb.at[0], rate_recv.at[0])

    def over_peers(act):
        def one(d, carry):
            act(d)
            return carry

        lax.fori_loop(1, RING, one, 0)

    def start_in(which, h):
        for a in which:
            own_block(a, h).start()
            over_peers(lambda d: incoming(a, h, d).start())

    def wait_in(which, h):
        for a in which:
            own_block(a, h).wait()
            over_peers(lambda d: incoming(a, h, d).wait_recv())

    own_rate.start()
    over_peers(lambda d: rates(d).start())

    def send_three(h, carry):
        start_in((0, 1, 2), h)
        return carry

    def send_query(h, carry):
        start_in((3,), h)
        return carry

    lax.fori_loop(0, HEADS, send_three, 0)
    lax.fori_loop(0, HEADS, send_query, 0)
    own_rate.wait()
    over_peers(lambda d: rates(d).wait_recv())

    def maps(h):
        spans[h, 0] = jnp.concatenate([jnp.where(eye, 1.0, 0.0), jnp.zeros((L, DK), F32)], 1)
        lane = lax.broadcasted_iota(jnp.int32, (L, rb.shape[2]), 1)
        mine = lane == z * HEADS + h

        def group(n, carry):
            pre = []
            for i in range(GROUP):
                b = n * GROUP + i
                slot = (z - b + RING) % RING
                rate = jnp.sum(
                    jnp.where(mine, rb[slot].astype(F32), 0.0), axis=1, keepdims=True
                )
                cum, mid, closing = running(gb[h, slot])
                kn = unit_rows(kb[h, slot].astype(F32))
                kr = kn * rate
                back = kr * jnp.exp(mid - cum)
                kp = kn * jnp.exp(cum)
                behind[h, b] = back
                past[h, b] = kp
                pre.append(
                    (
                        split(kn * jnp.exp(cum - mid)),
                        split(back),
                        split(kp),
                        split((kr * jnp.exp(closing - cum)).T),
                        jnp.where(eye, jnp.exp(closing), 0.0),
                        vb[h, slot],
                    )
                )
            among = [jnp.where(row > col, dot3(p[0], p[1], True), 0.0) for p in pre]
            inverse = unit_inverse(among)
            steps = []
            for i in range(GROUP):
                inv[h, n * GROUP + i] = inverse[i]
                reach = split(dot3(pre[i][3], split(inverse[i])))
                steps.append((pre[i][4] - dot3(reach, pre[i][2]), dot2(reach, pre[i][5])))
            prefix = spans[h, n * GROUP]
            for i in range(GROUP):
                prefix = compose(jnp.concatenate(steps[i], 1), prefix)
                spans[h, n * GROUP + i + 1] = prefix
            return carry

        lax.fori_loop(0, RING // GROUP, group, 0)

    def read_out(h, state):
        halves = split(state)

        def group(n, carry):
            entry, update = [], []
            for i in range(GROUP):
                b = n * GROUP + i
                slot = (z - b + RING) % RING
                span = spans[h, b]
                s = dot3(split(span[:, :DK]), halves) + span[:, DK:]
                entry.append(s)
            for i in range(GROUP):
                b = n * GROUP + i
                slot = (z - b + RING) % RING
                rest = vb[h, slot].astype(F32) - dot3(split(past[h, b]), split(entry[i]))
                update.append(dot3(split(inv[h, b]), split(rest)))
            for i in range(GROUP):
                b = n * GROUP + i
                slot = (z - b + RING) % RING
                cum, mid, closing = running(gb[h, slot])
                qn = unit_rows(qb[h, slot].astype(F32))
                attend = dot3(split(qn * jnp.exp(cum - mid)), split(behind[h, b]), True)
                attend = jnp.where(row >= col, attend, 0.0)
                left = jnp.concatenate([qn * jnp.exp(cum), attend], 1)
                right = jnp.concatenate([entry[i], update[i]], 0)
                l, r = split(left), split(right)
                out = mm(l[0], r[0]) + (mm(l[0], r[1]) + mm(l[1], r[0]))
                ob[h, (b - z + RING) % RING] = out.astype(BF)
            return carry

        lax.fori_loop(0, RING // GROUP, group, 0)

    def to_sibling(j):
        return remote(
            spans.at[2 * j + 1 - core, RING], sib.at[j], scan_send.at[j, 0], scan_recv.at[j, 0], (peer, z)
        )

    def to_x(j, d):
        return remote(
            chip.at[j], xb.at[j, d], scan_send.at[j, 1 + d], scan_recv.at[j, 1 + d], (x_peers[d], z)
        )

    def to_y(j, d):
        return remote(
            yb.at[j, 3], yb.at[j, d], scan_send.at[j, 4 + d], scan_recv.at[j, 4 + d], (y_peers[d], z)
        )

    def to_enter(j):
        return remote(
            enter.at[j, 1], enter.at[j, 2], scan_send.at[j, 7], scan_recv.at[j, 7], (peer, z)
        )

    def over_chip(j):
        to_sibling(j).wait_recv()
        own, other = spans[2 * j + core, RING], sib[j]
        first[j] = jnp.where(core == 0, own, other)
        chip[j] = compose(jnp.where(core == 0, other, own), first[j])
        for d in range(3):
            to_x(j, d).start()

    def over_x(j):
        for d in range(3):
            to_x(j, d).wait_recv()
        place = []
        for i in range(4):
            far = (x - i + 4) % 4
            place.append(
                jnp.where(
                    far == 0,
                    chip[j],
                    jnp.where(far == 1, xb[j, 0], jnp.where(far == 2, xb[j, 1], xb[j, 2])),
                )
            )
        two = compose(place[1], place[0])
        yb[j, 3] = compose(compose(place[3], place[2]), two)
        for d in range(3):
            to_y(j, d).start()
        three = compose(place[2], two)
        before[j] = jnp.where(
            x == 0,
            spans[0, 0],
            jnp.where(x == 1, place[0], jnp.where(x == 2, two, three)),
        )

    def over_y(j):
        for d in range(3):
            to_y(j, d).wait_recv()
        place = []
        for i in range(3):
            far = (y - i + 4) % 4
            place.append(
                jnp.where(
                    far == 0,
                    yb[j, 3],
                    jnp.where(far == 1, yb[j, 0], jnp.where(far == 2, yb[j, 1], yb[j, 2])),
                )
            )
        one = place[0][:, DK:]
        two = advance(place[1], one)
        three = advance(place[2], two)
        state = jnp.where(y == 0, 0.0, jnp.where(y == 1, one, jnp.where(y == 2, two, three)))
        state = advance(before[j], state)
        after = advance(first[j], state)
        enter[j, 0] = jnp.where(core == 0, state, after)
        enter[j, 1] = jnp.where(core == 0, after, state)
        to_enter(j).start()

    def turn_in(h, carry):
        pl.when(h == 2)(lambda: over_chip(0))
        wait_in((0, 1, 2), h)
        maps(h)
        pl.when(h == 1)(lambda: to_sibling(0).start())
        pl.when(h == 2)(lambda: over_x(0))
        pl.when(h == 3)(lambda: to_sibling(1).start())
        return carry

    lax.fori_loop(0, HEADS, turn_in, 0)

    def turn_out(h, carry):
        @pl.when(h == 0)
        def _():
            over_y(0)
            over_chip(1)
            to_enter(0).wait_recv()

        pl.when(h == 1)(lambda: over_x(1))

        @pl.when(h == 2)
        def _():
            over_y(1)
            to_enter(1).wait_recv()

        wait_in((3,), h)
        j, half = h // 2, h % 2
        read_out(h, jnp.where(core == half, enter[j, 0], enter[j, 2]))
        own_out(h).start()
        over_peers(lambda d: outgoing(h, d).start())
        return carry

    lax.fori_loop(0, HEADS, turn_out, 0)

    def finish(h, carry):
        own_out(h).wait()
        over_peers(lambda d: outgoing(h, d).wait())
        for a in range(4):
            over_peers(lambda d: incoming(a, h, d).wait_send())
        return carry

    lax.fori_loop(0, HEADS, finish, 0)
    over_peers(lambda d: rates(d).wait_send())
    for j in range(2):
        to_sibling(j).wait_send()
        to_enter(j).wait_send()
        for d in range(3):
            to_x(j, d).wait_send()
            to_y(j, d).wait_send()


def local(query_rows, key_rows, value_rows, log_decay, write_rate):
    rows, heads = write_rate.shape
    anywhere = pl.BlockSpec(memory_space=pl.ANY)
    block = pltpu.VMEM((HEADS, RING, L, DK), BF)
    wide = pltpu.VMEM((HEADS, RING, L, DK), F32)
    pair = pltpu.VMEM((2, DK, 2 * DK), F32)
    return pl.pallas_call(
        kernel,
        in_specs=[anywhere] * 5,
        out_specs=anywhere,
        out_shape=jax.ShapeDtypeStruct(query_rows.shape, BF),
        scratch_shapes=[
            block,
            block,
            block,
            block,
            pltpu.VMEM((RING, rows, heads), BF),
            block,
            wide,
            wide,
            wide,
            pltpu.VMEM((HEADS, RING + 1, DK, 2 * DK), F32),
            pair,
            pair,
            pair,
            pltpu.VMEM((2, 3, DK, 2 * DK), F32),
            pair,
            pltpu.VMEM((2, 4, DK, 2 * DK), F32),
            pltpu.VMEM((2, 3, DK, DK), F32),
            pltpu.SemaphoreType.DMA((4, HEADS, RING)),
            pltpu.SemaphoreType.DMA((4, HEADS, RING)),
            pltpu.SemaphoreType.DMA((HEADS, RING)),
            pltpu.SemaphoreType.DMA((HEADS, RING)),
            pltpu.SemaphoreType.DMA((RING,)),
            pltpu.SemaphoreType.DMA((RING,)),
            pltpu.SemaphoreType.DMA((2, 8)),
            pltpu.SemaphoreType.DMA((2, 8)),
        ],
        compiler_params=pltpu.CompilerParams(
            vmem_limit_bytes=48 * 2**20, collective_id=0, has_side_effects=True
        ),
    )(query_rows, key_rows, value_rows, log_decay, write_rate)


def solution(mesh):
    spec = P(("seq", "head"), None)
    return jax.shard_map(
        local, mesh=mesh, in_specs=(spec,) * 5, out_specs=spec, check_vma=False
    )
```

```python
import functools

import jax
import jax.numpy as jnp
from jax import lax
from jax.experimental import pallas as pl
from jax.experimental.pallas import tpu as pltpu
from jax.sharding import PartitionSpec as P

DK = 128
L = 128
RING = 8
LIMIT = 52
HEADS = 4
GROUP = 4
F32 = jnp.float32
BF = jnp.bfloat16
MESH = pl.DeviceIdType.MESH


def split(x):
    hi = x.astype(BF)
    return hi, (x - hi.astype(F32)).astype(BF)


def mm(a, b, dims=((1,), (0,))):
    return lax.dot_general(a, b, (dims, ((), ())), preferred_element_type=F32)


def dot3(a, b, turned=False):
    dims = ((1,), (1,)) if turned else ((1,), (0,))
    wide = jnp.concatenate([a[0], a[1]], 1)
    twice = jnp.concatenate([b[0], b[0]], 1 if turned else 0)
    return mm(wide, twice, dims) + mm(a[0], b[1], dims)


def dot2(a, b):
    return mm(jnp.concatenate([a[0], a[1]], 1), jnp.concatenate([b, b], 0))


def unit_rows(x):
    return x * lax.rsqrt(jnp.sum(x * x, axis=-1, keepdims=True) + 1e-6)


def masks():
    row = lax.broadcasted_iota(jnp.int32, (L, L), 0)
    col = lax.broadcasted_iota(jnp.int32, (L, L), 1)
    return row, col


def unit_inverse(among):
    row, col = masks()
    eye = jnp.where(row == col, 1.0, 0.0)
    inverse = None
    size = 1
    while size < L:
        lower = jnp.logical_and(
            row // (2 * size) == col // (2 * size),
            jnp.logical_and((row // size) % 2 == 1, (col // size) % 2 == 0),
        )
        if inverse is None:
            inverse = [eye - jnp.where(lower, a, 0.0) for a in among]
        else:
            halves = [split(x) for x in inverse]
            right = [
                split(dot3(split(jnp.where(lower, a, 0.0)), x)) for a, x in zip(among, halves)
            ]
            inverse = [x - dot3(h, r) for x, h, r in zip(inverse, halves, right)]
        size *= 2
    return inverse


def running(g):
    row, col = masks()
    cum = mm((row >= col).astype(BF), g)
    return cum, cum[L // 2 : L // 2 + 1, :], cum[L - 1 : L, :]


def compose(later, earlier):
    product = dot3(split(later[:, :DK]), split(earlier))
    return jnp.concatenate([product[:, :DK], product[:, DK:] + later[:, DK:]], 1)


def advance(span, state):
    return dot3(split(span[:, :DK]), split(state)) + span[:, DK:]


def kernel(
    q_ref, k_ref, v_ref, g_ref, rate_ref, out_ref,
    kb, gb, vb, qb, rb, ob, inv, past, behind, weight, spans,
    sib, chip, first, xb, before, yb, enter,
    in_send, in_recv, out_send, out_recv, rate_send, rate_recv, scan_send, scan_recv,
):
    me = lax.axis_index("seq")
    z = lax.axis_index("head")
    core, x, y = me % 2, (me // 2) % 4, me // 8
    peer = me + 1 - 2 * core
    x_peers = [y * 8 + ((x + d) % 4) * 2 + core for d in (1, 2, 3)]
    y_peers = [((y + d) % 4) * 8 + x * 2 + core for d in (1, 2, 3)]
    row, col = masks()
    eye = row == col

    barrier = pltpu.get_barrier_semaphore()

    def greet(d, carry):
        pl.semaphore_signal(barrier, inc=1, device_id=(me, (z + d) % RING), device_id_type=MESH)
        return carry

    lax.fori_loop(1, RING, greet, 0)
    for to in [peer] + x_peers + y_peers:
        pl.semaphore_signal(barrier, inc=1, device_id=(to, z), device_id_type=MESH)
    pl.semaphore_wait(barrier, RING + 6)

    def columns(owner, h):
        return pl.ds(pl.multiple_of((owner * HEADS + h) * DK, DK), DK)

    def remote(src, dst, send, recv, to):
        return pltpu.make_async_remote_copy(
            src_ref=src, dst_ref=dst, send_sem=send, recv_sem=recv, device_id=to, device_id_type=MESH
        )

    arrays = ((k_ref, kb), (g_ref, gb), (v_ref, vb), (q_ref, qb))

    def incoming(a, h, d):
        to = (z + d) % RING
        src, dst = arrays[a]
        return remote(
            src.at[:, columns(to, h)], dst.at[h, d], in_send.at[a, h, d], in_recv.at[a, h, d], (me, to)
        )

    def own_block(a, h):
        src, dst = arrays[a]
        return pltpu.make_async_copy(src.at[:, columns(z, h)], dst.at[h, 0], in_recv.at[a, h, 0])

    def rates(d):
        to = (z + d) % RING
        return remote(rate_ref, rb.at[d], rate_send.at[d], rate_recv.at[d], (me, to))

    def outgoing(h, d):
        to = (z + d) % RING
        return remote(
            ob.at[h, d], out_ref.at[:, columns(z, h)], out_send.at[h, d], out_recv.at[h, d], (me, to)
        )

    def own_out(h):
        return pltpu.make_async_copy(ob.at[h, 0], out_ref.at[:, columns(z, h)], out_recv.at[h, 0])

    own_rate = pltpu.make_async_copy(rate_ref, rb.at[0], rate_recv.at[0])

    def over_peers(act):
        def one(d, carry):
            act(d)
            return carry

        lax.fori_loop(1, RING, one, 0)

    def start_in(which, h):
        for a in which:
            own_block(a, h).start()
            over_peers(lambda d: incoming(a, h, d).start())

    def wait_in(which, h):
        for a in which:
            own_block(a, h).wait()
            over_peers(lambda d: incoming(a, h, d).wait_recv())

    own_rate.start()
    over_peers(lambda d: rates(d).start())

    def send_three(h, carry):
        start_in((0, 1, 2), h)
        return carry

    def send_query(h, carry):
        start_in((3,), h)
        return carry

    lax.fori_loop(0, HEADS, send_three, 0)
    lax.fori_loop(0, HEADS, send_query, 0)
    own_rate.wait()
    over_peers(lambda d: rates(d).wait_recv())

    def maps(h):
        spans[h, 0] = jnp.concatenate([jnp.where(eye, 1.0, 0.0), jnp.zeros((L, DK), F32)], 1)
        mine = lax.broadcasted_iota(jnp.int32, rb.shape[1:], 0) == z * HEADS + h

        def group(n, carry):
            pre = []
            for i in range(GROUP):
                b = n * GROUP + i
                slot = (z - b + RING) % RING
                rate = jnp.sum(jnp.where(mine, rb[slot].astype(F32), 0.0), axis=0, keepdims=True)
                weight[h, b] = rate
                cum, mid, closing = running(gb[h, slot])
                kn = unit_rows(kb[h, slot].astype(F32))
                back = kn * jnp.exp(mid - cum)
                kp = kn * jnp.exp(cum)
                behind[h, b] = back
                past[h, b] = kp
                pre.append(
                    (
                        split(kn * jnp.exp(cum - mid)),
                        split(back),
                        split(kp),
                        split((kn * jnp.exp(closing - cum)).T * rate),
                        jnp.where(eye, jnp.exp(closing), 0.0),
                        vb[h, slot],
                        rate,
                    )
                )
            among = [jnp.where(row > col, dot3(p[0], p[1], True), 0.0) * p[6] for p in pre]
            inverse = unit_inverse(among)
            steps = []
            for i in range(GROUP):
                inv[h, n * GROUP + i] = inverse[i]
                reach = split(dot3(pre[i][3], split(inverse[i])))
                steps.append((pre[i][4] - dot3(reach, pre[i][2]), dot2(reach, pre[i][5])))
            prefix = spans[h, n * GROUP]
            for i in range(GROUP):
                prefix = compose(jnp.concatenate(steps[i], 1), prefix)
                spans[h, n * GROUP + i + 1] = prefix
            return carry

        lax.fori_loop(0, RING // GROUP, group, 0)

    def read_out(h, state):
        halves = split(state)

        def group(n, carry):
            entry, update = [], []
            for i in range(GROUP):
                b = n * GROUP + i
                slot = (z - b + RING) % RING
                span = spans[h, b]
                s = dot3(split(span[:, :DK]), halves) + span[:, DK:]
                entry.append(s)
            for i in range(GROUP):
                b = n * GROUP + i
                slot = (z - b + RING) % RING
                rest = vb[h, slot].astype(F32) - dot3(split(past[h, b]), split(entry[i]))
                update.append(dot3(split(inv[h, b]), split(rest)))
            for i in range(GROUP):
                b = n * GROUP + i
                slot = (z - b + RING) % RING
                cum, mid, closing = running(gb[h, slot])
                qn = unit_rows(qb[h, slot].astype(F32))
                attend = dot3(split(qn * jnp.exp(cum - mid)), split(behind[h, b]), True)
                attend = jnp.where(row >= col, attend, 0.0) * weight[h, b]
                left = jnp.concatenate([qn * jnp.exp(cum), attend], 1)
                right = jnp.concatenate([entry[i], update[i]], 0)
                l, r = split(left), split(right)
                out = mm(l[0], r[0]) + (mm(l[0], r[1]) + mm(l[1], r[0]))
                ob[h, (b - z + RING) % RING] = out.astype(BF)
            for i in range(GROUP):
                d = (n * GROUP + i - z + RING) % RING
                pl.when(d == 0)(lambda: own_out(h).start())
                pl.when(d != 0)(lambda d=d: outgoing(h, d).start())
            return carry

        lax.fori_loop(0, RING // GROUP, group, 0)

    def to_sibling(j):
        return remote(
            spans.at[2 * j + 1 - core, RING], sib.at[j], scan_send.at[j, 0], scan_recv.at[j, 0], (peer, z)
        )

    def to_x(j, d):
        return remote(
            chip.at[j], xb.at[j, d], scan_send.at[j, 1 + d], scan_recv.at[j, 1 + d], (x_peers[d], z)
        )

    def to_y(j, d):
        return remote(
            yb.at[j, 3], yb.at[j, d], scan_send.at[j, 4 + d], scan_recv.at[j, 4 + d], (y_peers[d], z)
        )

    def to_enter(j):
        return remote(
            enter.at[j, 1], enter.at[j, 2], scan_send.at[j, 7], scan_recv.at[j, 7], (peer, z)
        )

    def over_chip(j):
        to_sibling(j).wait_recv()
        own, other = spans[2 * j + core, RING], sib[j]
        first[j] = jnp.where(core == 0, own, other)
        chip[j] = compose(jnp.where(core == 0, other, own), first[j])
        for d in range(3):
            to_x(j, d).start()

    def over_x(j):
        for d in range(3):
            to_x(j, d).wait_recv()
        place = []
        for i in range(4):
            far = (x - i + 4) % 4
            place.append(
                jnp.where(
                    far == 0,
                    chip[j],
                    jnp.where(far == 1, xb[j, 0], jnp.where(far == 2, xb[j, 1], xb[j, 2])),
                )
            )
        two = compose(place[1], place[0])
        yb[j, 3] = compose(compose(place[3], place[2]), two)
        for d in range(3):
            to_y(j, d).start()
        three = compose(place[2], two)
        before[j] = jnp.where(
            x == 0,
            spans[0, 0],
            jnp.where(x == 1, place[0], jnp.where(x == 2, two, three)),
        )

    def over_y(j):
        for d in range(3):
            to_y(j, d).wait_recv()
        place = []
        for i in range(3):
            far = (y - i + 4) % 4
            place.append(
                jnp.where(
                    far == 0,
                    yb[j, 3],
                    jnp.where(far == 1, yb[j, 0], jnp.where(far == 2, yb[j, 1], yb[j, 2])),
                )
            )
        one = place[0][:, DK:]
        two = advance(place[1], one)
        three = advance(place[2], two)
        state = jnp.where(y == 0, 0.0, jnp.where(y == 1, one, jnp.where(y == 2, two, three)))
        state = advance(before[j], state)
        after = advance(first[j], state)
        enter[j, 0] = jnp.where(core == 0, state, after)
        enter[j, 1] = jnp.where(core == 0, after, state)
        to_enter(j).start()

    def turn_in(h, carry):
        pl.when(h == 2)(lambda: over_chip(0))
        wait_in((0, 1, 2), h)
        maps(h)
        pl.when(h == 1)(lambda: to_sibling(0).start())
        pl.when(h == 2)(lambda: over_x(0))
        pl.when(h == 3)(lambda: to_sibling(1).start())
        return carry

    lax.fori_loop(0, HEADS, turn_in, 0)

    def turn_out(h, carry):
        @pl.when(h == 0)
        def _():
            over_y(0)
            over_chip(1)
            to_enter(0).wait_recv()

        pl.when(h == 1)(lambda: over_x(1))

        @pl.when(h == 2)
        def _():
            over_y(1)
            to_enter(1).wait_recv()

        wait_in((3,), h)
        j, half = h // 2, h % 2
        read_out(h, jnp.where(core == half, enter[j, 0], enter[j, 2]))
        return carry

    lax.fori_loop(0, HEADS, turn_out, 0)

    def finish(h, carry):
        own_out(h).wait()
        over_peers(lambda d: outgoing(h, d).wait())
        for a in range(4):
            over_peers(lambda d: incoming(a, h, d).wait_send())
        return carry

    lax.fori_loop(0, HEADS, finish, 0)
    over_peers(lambda d: rates(d).wait_send())
    for j in range(2):
        to_sibling(j).wait_send()
        to_enter(j).wait_send()
        for d in range(3):
            to_x(j, d).wait_send()
            to_y(j, d).wait_send()


def local(query_rows, key_rows, value_rows, log_decay, write_rate):
    rows, heads = write_rate.shape
    anywhere = pl.BlockSpec(memory_space=pltpu.HBM)
    block = pltpu.VMEM((HEADS, RING, L, DK), BF)
    wide = pltpu.VMEM((HEADS, RING, L, DK), F32)
    pair = pltpu.VMEM((2, DK, 2 * DK), F32)
    return pl.pallas_call(
        kernel,
        in_specs=[anywhere] * 5,
        out_specs=pl.BlockSpec(memory_space=pltpu.VMEM),
        out_shape=jax.ShapeDtypeStruct(query_rows.shape, BF),
        scratch_shapes=[
            block,
            block,
            block,
            block,
            pltpu.VMEM((RING, heads, rows), BF),
            block,
            wide,
            wide,
            wide,
            pltpu.VMEM((HEADS, RING, 1, L), F32),
            pltpu.VMEM((HEADS, RING + 1, DK, 2 * DK), F32),
            pair,
            pair,
            pair,
            pltpu.VMEM((2, 3, DK, 2 * DK), F32),
            pair,
            pltpu.VMEM((2, 4, DK, 2 * DK), F32),
            pltpu.VMEM((2, 3, DK, DK), F32),
            pltpu.SemaphoreType.DMA((4, HEADS, RING)),
            pltpu.SemaphoreType.DMA((4, HEADS, RING)),
            pltpu.SemaphoreType.DMA((HEADS, RING)),
            pltpu.SemaphoreType.DMA((HEADS, RING)),
            pltpu.SemaphoreType.DMA((RING,)),
            pltpu.SemaphoreType.DMA((RING,)),
            pltpu.SemaphoreType.DMA((2, 8)),
            pltpu.SemaphoreType.DMA((2, 8)),
        ],
        compiler_params=pltpu.CompilerParams(
            vmem_limit_bytes=LIMIT * 2**20, collective_id=0, has_side_effects=True
        ),
    )(query_rows, key_rows, value_rows, log_decay, write_rate.T)


def solution(mesh):
    spec = P(("seq", "head"), None)
    return jax.shard_map(
        local, mesh=mesh, in_specs=(spec,) * 5, out_specs=spec, check_vma=False
    )
```

```python
import functools

import jax
import jax.numpy as jnp
from jax import lax
from jax.experimental import pallas as pl
from jax.experimental.pallas import tpu as pltpu
from jax.sharding import PartitionSpec as P

DK = 128
L = 128
RING = 8
LIMIT = 52
HEADS = 4
GROUP = 4
F32 = jnp.float32
BF = jnp.bfloat16
MESH = pl.DeviceIdType.MESH


def split(x):
    hi = x.astype(BF)
    return hi, (x - hi.astype(F32)).astype(BF)


def mm(a, b, dims=((1,), (0,))):
    return lax.dot_general(a, b, (dims, ((), ())), preferred_element_type=F32)


def dot3(a, b, turned=False):
    dims = ((1,), (1,)) if turned else ((1,), (0,))
    wide = jnp.concatenate([a[0], a[1]], 1)
    twice = jnp.concatenate([b[0], b[0]], 1 if turned else 0)
    return mm(wide, twice, dims) + mm(a[0], b[1], dims)


def dot2(a, b):
    return mm(jnp.concatenate([a[0], a[1]], 1), jnp.concatenate([b, b], 0))


def unit_rows(x):
    return x * lax.rsqrt(jnp.sum(x * x, axis=-1, keepdims=True) + 1e-6)


def masks():
    row = lax.broadcasted_iota(jnp.int32, (L, L), 0)
    col = lax.broadcasted_iota(jnp.int32, (L, L), 1)
    return row, col


def unit_inverse(among):
    row, col = masks()
    eye = jnp.where(row == col, 1.0, 0.0)
    inverse = None
    size = 1
    while size < L:
        lower = jnp.logical_and(
            row // (2 * size) == col // (2 * size),
            jnp.logical_and((row // size) % 2 == 1, (col // size) % 2 == 0),
        )
        if inverse is None:
            inverse = [eye - jnp.where(lower, a, 0.0) for a in among]
        else:
            halves = [split(x) for x in inverse]
            right = [
                split(dot3(split(jnp.where(lower, a, 0.0)), x)) for a, x in zip(among, halves)
            ]
            inverse = [x - dot3(h, r) for x, h, r in zip(inverse, halves, right)]
        size *= 2
    return inverse


def running(g):
    row, col = masks()
    cum = mm((row >= col).astype(BF), g)
    return cum, cum[L // 2 : L // 2 + 1, :], cum[L - 1 : L, :]


def compose(later, earlier):
    product = dot3(split(later[:, :DK]), split(earlier))
    return jnp.concatenate([product[:, :DK], product[:, DK:] + later[:, DK:]], 1)


def advance(span, state):
    return dot3(split(span[:, :DK]), split(state)) + span[:, DK:]


def kernel(
    q_ref, k_ref, v_ref, g_ref, rate_ref, out_ref,
    kb, gb, vb, qb, rb, ob, inv, past, behind, weight, spans,
    sib, chip, first, xb, before, yb, enter,
    in_send, in_recv, out_send, out_recv, rate_send, rate_recv, scan_send, scan_recv,
):
    me = lax.axis_index("seq")
    z = lax.axis_index("head")
    core, x, y = me % 2, (me // 2) % 4, me // 8
    peer = me + 1 - 2 * core
    x_peers = [y * 8 + ((x + d) % 4) * 2 + core for d in (1, 2, 3)]
    y_peers = [((y + d) % 4) * 8 + x * 2 + core for d in (1, 2, 3)]
    row, col = masks()
    eye = row == col

    barrier = pltpu.get_barrier_semaphore()

    def greet(d, carry):
        pl.semaphore_signal(barrier, inc=1, device_id=(me, (z + d) % RING), device_id_type=MESH)
        return carry

    lax.fori_loop(1, RING, greet, 0)
    for to in [peer] + x_peers + y_peers:
        pl.semaphore_signal(barrier, inc=1, device_id=(to, z), device_id_type=MESH)
    pl.semaphore_wait(barrier, RING + 6)

    def columns(owner, h):
        return pl.ds(pl.multiple_of((owner * HEADS + h) * DK, DK), DK)

    def remote(src, dst, send, recv, to):
        return pltpu.make_async_remote_copy(
            src_ref=src, dst_ref=dst, send_sem=send, recv_sem=recv, device_id=to, device_id_type=MESH
        )

    arrays = ((k_ref, kb), (g_ref, gb), (v_ref, vb), (q_ref, qb))

    def incoming(a, h, d):
        to = (z + d) % RING
        src, dst = arrays[a]
        return remote(
            src.at[:, columns(to, h)], dst.at[h, d], in_send.at[a, h, d], in_recv.at[a, h, d], (me, to)
        )

    def own_block(a, h):
        src, dst = arrays[a]
        return pltpu.make_async_copy(src.at[:, columns(z, h)], dst.at[h, 0], in_recv.at[a, h, 0])

    def rates(d):
        to = (z + d) % RING
        return remote(rate_ref, rb.at[d], rate_send.at[d], rate_recv.at[d], (me, to))

    def outgoing(h, d):
        to = (z + d) % RING
        return remote(
            ob.at[h, d], out_ref.at[:, columns(z, h)], out_send.at[h, d], out_recv.at[h, d], (me, to)
        )

    def own_out(h):
        return pltpu.make_async_copy(ob.at[h, 0], out_ref.at[:, columns(z, h)], out_recv.at[h, 0])

    own_rate = pltpu.make_async_copy(rate_ref, rb.at[0], rate_recv.at[0])

    def over_peers(act):
        def one(d, carry):
            act(d)
            return carry

        lax.fori_loop(1, RING, one, 0)

    def start_in(which, h):
        for a in which:
            own_block(a, h).start()
            over_peers(lambda d: incoming(a, h, d).start())

    def wait_in(which, h):
        for a in which:
            own_block(a, h).wait()
            over_peers(lambda d: incoming(a, h, d).wait_recv())

    own_rate.start()
    over_peers(lambda d: rates(d).start())

    def send_three(h, carry):
        start_in((0, 1, 2), h)
        return carry

    def send_query(h, carry):
        start_in((3,), h)
        return carry

    lax.fori_loop(0, HEADS, send_three, 0)
    lax.fori_loop(0, HEADS, send_query, 0)
    own_rate.wait()
    over_peers(lambda d: rates(d).wait_recv())

    def maps(h):
        spans[h, 0] = jnp.concatenate([jnp.where(eye, 1.0, 0.0), jnp.zeros((L, DK), F32)], 1)
        mine = lax.broadcasted_iota(jnp.int32, rb.shape[1:], 0) == z * HEADS + h

        def group(n, carry):
            pre = []
            for i in range(RING):
                b = n * RING + i
                slot = (z - b + RING) % RING
                rate = jnp.sum(jnp.where(mine, rb[slot].astype(F32), 0.0), axis=0, keepdims=True)
                weight[h, b] = rate
                cum, mid, closing = running(gb[h, slot])
                kn = unit_rows(kb[h, slot].astype(F32))
                back = kn * jnp.exp(mid - cum)
                kp = kn * jnp.exp(cum)
                behind[h, b] = back
                past[h, b] = kp
                pre.append(
                    (
                        split(kn * jnp.exp(cum - mid)),
                        split(back),
                        split(kp),
                        split((kn * jnp.exp(closing - cum)).T * rate),
                        jnp.where(eye, jnp.exp(closing), 0.0),
                        vb[h, slot],
                        rate,
                    )
                )
            among = [jnp.where(row > col, dot3(p[0], p[1], True), 0.0) * p[6] for p in pre]
            inverse = unit_inverse(among)
            steps = []
            for i in range(RING):
                inv[h, n * RING + i] = inverse[i]
                reach = split(dot3(pre[i][3], split(inverse[i])))
                steps.append((pre[i][4] - dot3(reach, pre[i][2]), dot2(reach, pre[i][5])))
            prefix = spans[h, n * RING]
            for i in range(RING):
                prefix = compose(jnp.concatenate(steps[i], 1), prefix)
                spans[h, n * RING + i + 1] = prefix
            return carry

        group(0, 0)

    def read_out(h, state):
        halves = split(state)

        def group(n, carry):
            entry, update = [], []
            for i in range(GROUP):
                b = n * GROUP + i
                slot = (z - b + RING) % RING
                span = spans[h, b]
                s = dot3(split(span[:, :DK]), halves) + span[:, DK:]
                entry.append(s)
            for i in range(GROUP):
                b = n * GROUP + i
                slot = (z - b + RING) % RING
                rest = vb[h, slot].astype(F32) - dot3(split(past[h, b]), split(entry[i]))
                update.append(dot3(split(inv[h, b]), split(rest)))
            for i in range(GROUP):
                b = n * GROUP + i
                slot = (z - b + RING) % RING
                cum, mid, closing = running(gb[h, slot])
                qn = unit_rows(qb[h, slot].astype(F32))
                attend = dot3(split(qn * jnp.exp(cum - mid)), split(behind[h, b]), True)
                attend = jnp.where(row >= col, attend, 0.0) * weight[h, b]
                left = jnp.concatenate([qn * jnp.exp(cum), attend], 1)
                right = jnp.concatenate([entry[i], update[i]], 0)
                l, r = split(left), split(right)
                out = mm(l[0], r[0]) + (mm(l[0], r[1]) + mm(l[1], r[0]))
                ob[h, (b - z + RING) % RING] = out.astype(BF)
            for i in range(GROUP):
                d = (n * GROUP + i - z + RING) % RING
                pl.when(d == 0)(lambda: own_out(h).start())
                pl.when(d != 0)(lambda d=d: outgoing(h, d).start())
            return carry

        lax.fori_loop(0, RING // GROUP, group, 0)

    def to_sibling(j):
        return remote(
            spans.at[2 * j + 1 - core, RING], sib.at[j], scan_send.at[j, 0], scan_recv.at[j, 0], (peer, z)
        )

    def to_x(j, d):
        return remote(
            chip.at[j], xb.at[j, d], scan_send.at[j, 1 + d], scan_recv.at[j, 1 + d], (x_peers[d], z)
        )

    def to_y(j, d):
        return remote(
            yb.at[j, 3], yb.at[j, d], scan_send.at[j, 4 + d], scan_recv.at[j, 4 + d], (y_peers[d], z)
        )

    def on_y(j, start):
        for d in range(3):
            if start:
                pl.when(y + d + 1 < 4)(lambda d=d: to_y(j, d).start())
            else:
                pl.when(y >= d + 1)(lambda d=d: to_y(j, d).wait_recv())

    def to_enter(j):
        return remote(
            enter.at[j, 1], enter.at[j, 2], scan_send.at[j, 7], scan_recv.at[j, 7], (peer, z)
        )

    def over_chip(j):
        to_sibling(j).wait_recv()
        own, other = spans[2 * j + core, RING], sib[j]
        first[j] = jnp.where(core == 0, own, other)
        chip[j] = compose(jnp.where(core == 0, other, own), first[j])
        for d in range(3):
            to_x(j, d).start()

    def over_x(j):
        for d in range(3):
            to_x(j, d).wait_recv()
        place = []
        for i in range(4):
            far = (x - i + 4) % 4
            place.append(
                jnp.where(
                    far == 0,
                    chip[j],
                    jnp.where(far == 1, xb[j, 0], jnp.where(far == 2, xb[j, 1], xb[j, 2])),
                )
            )
        two = compose(place[1], place[0])
        yb[j, 3] = compose(compose(place[3], place[2]), two)
        on_y(j, True)
        three = compose(place[2], two)
        before[j] = jnp.where(
            x == 0,
            spans[0, 0],
            jnp.where(x == 1, place[0], jnp.where(x == 2, two, three)),
        )

    def over_y(j):
        on_y(j, False)
        place = []
        for i in range(3):
            far = (y - i + 4) % 4
            place.append(
                jnp.where(
                    far == 0,
                    yb[j, 3],
                    jnp.where(far == 1, yb[j, 0], jnp.where(far == 2, yb[j, 1], yb[j, 2])),
                )
            )
        one = place[0][:, DK:]
        two = advance(place[1], one)
        three = advance(place[2], two)
        state = jnp.where(y == 0, 0.0, jnp.where(y == 1, one, jnp.where(y == 2, two, three)))
        state = advance(before[j], state)
        after = advance(first[j], state)
        enter[j, 0] = jnp.where(core == 0, state, after)
        enter[j, 1] = jnp.where(core == 0, after, state)
        to_enter(j).start()

    def turn_in(h, carry):
        pl.when(h == 2)(lambda: over_chip(0))
        wait_in((0, 1, 2), h)
        maps(h)
        pl.when(h == 1)(lambda: to_sibling(0).start())
        pl.when(h == 2)(lambda: over_x(0))
        pl.when(h == 3)(lambda: to_sibling(1).start())
        return carry

    lax.fori_loop(0, HEADS, turn_in, 0)

    def turn_out(h, carry):
        @pl.when(h == 0)
        def _():
            over_y(0)
            over_chip(1)
            to_enter(0).wait_recv()

        pl.when(h == 1)(lambda: over_x(1))

        @pl.when(h == 2)
        def _():
            over_y(1)
            to_enter(1).wait_recv()

        wait_in((3,), h)
        j, half = h // 2, h % 2
        read_out(h, jnp.where(core == half, enter[j, 0], enter[j, 2]))
        return carry

    lax.fori_loop(0, HEADS, turn_out, 0)

    def finish(h, carry):
        own_out(h).wait()
        over_peers(lambda d: outgoing(h, d).wait())
        for a in range(4):
            over_peers(lambda d: incoming(a, h, d).wait_send())
        return carry

    lax.fori_loop(0, HEADS, finish, 0)
    over_peers(lambda d: rates(d).wait_send())
    for j in range(2):
        to_sibling(j).wait_send()
        to_enter(j).wait_send()
        for d in range(3):
            to_x(j, d).wait_send()
            pl.when(y + d + 1 < 4)(lambda d=d: to_y(j, d).wait_send())


def local(query_rows, key_rows, value_rows, log_decay, write_rate):
    rows, heads = write_rate.shape
    anywhere = pl.BlockSpec(memory_space=pltpu.HBM)
    block = pltpu.VMEM((HEADS, RING, L, DK), BF)
    wide = pltpu.VMEM((HEADS, RING, L, DK), F32)
    pair = pltpu.VMEM((2, DK, 2 * DK), F32)
    return pl.pallas_call(
        kernel,
        in_specs=[anywhere] * 5,
        out_specs=pl.BlockSpec(memory_space=pltpu.VMEM),
        out_shape=jax.ShapeDtypeStruct(query_rows.shape, BF),
        scratch_shapes=[
            block,
            block,
            block,
            block,
            pltpu.VMEM((RING, heads, rows), BF),
            block,
            wide,
            wide,
            wide,
            pltpu.VMEM((HEADS, RING, 1, L), F32),
            pltpu.VMEM((HEADS, RING + 1, DK, 2 * DK), F32),
            pair,
            pair,
            pair,
            pltpu.VMEM((2, 3, DK, 2 * DK), F32),
            pair,
            pltpu.VMEM((2, 4, DK, 2 * DK), F32),
            pltpu.VMEM((2, 3, DK, DK), F32),
            pltpu.SemaphoreType.DMA((4, HEADS, RING)),
            pltpu.SemaphoreType.DMA((4, HEADS, RING)),
            pltpu.SemaphoreType.DMA((HEADS, RING)),
            pltpu.SemaphoreType.DMA((HEADS, RING)),
            pltpu.SemaphoreType.DMA((RING,)),
            pltpu.SemaphoreType.DMA((RING,)),
            pltpu.SemaphoreType.DMA((2, 8)),
            pltpu.SemaphoreType.DMA((2, 8)),
        ],
        compiler_params=pltpu.CompilerParams(
            vmem_limit_bytes=LIMIT * 2**20, collective_id=0, has_side_effects=True
        ),
    )(query_rows, key_rows, value_rows, log_decay, write_rate.T)


def solution(mesh):
    spec = P(("seq", "head"), None)
    return jax.shard_map(
        local, mesh=mesh, in_specs=(spec,) * 5, out_specs=spec, check_vma=False
    )
```

```python
import functools

import jax
import jax.numpy as jnp
from jax import lax
from jax.experimental import pallas as pl
from jax.experimental.pallas import tpu as pltpu
from jax.sharding import PartitionSpec as P

DK = 128
L = 128
RING = 8
LIMIT = 52
HEADS = 4
GROUP = 4
F32 = jnp.float32
BF = jnp.bfloat16
MESH = pl.DeviceIdType.MESH


def split(x):
    hi = x.astype(BF)
    return hi, (x - hi.astype(F32)).astype(BF)


def mm(a, b, dims=((1,), (0,))):
    return lax.dot_general(a, b, (dims, ((), ())), preferred_element_type=F32)


def dot3(a, b, turned=False):
    wide = jnp.concatenate([a[0], a[1]], 1)
    if turned:
        both = jnp.concatenate([b[0], b[1]], 0)
        product = mm(wide, jnp.concatenate([both, both], 1), ((1,), (1,)))
    else:
        both = jnp.concatenate([b[0], b[1]], 1)
        product = mm(wide, jnp.concatenate([both, both], 0))
    half = product.shape[1] // 2
    return product[:, :half] + product[:, half:]


def dot2(a, b):
    return mm(jnp.concatenate([a[0], a[1]], 1), jnp.concatenate([b, b], 0))


def unit_rows(x):
    return x * lax.rsqrt(jnp.sum(x * x, axis=-1, keepdims=True) + 1e-6)


def masks():
    row = lax.broadcasted_iota(jnp.int32, (L, L), 0)
    col = lax.broadcasted_iota(jnp.int32, (L, L), 1)
    return row, col


def unit_inverse(among):
    row, col = masks()
    eye = jnp.where(row == col, 1.0, 0.0)
    inverse = None
    size = 1
    while size < L:
        lower = jnp.logical_and(
            row // (2 * size) == col // (2 * size),
            jnp.logical_and((row // size) % 2 == 1, (col // size) % 2 == 0),
        )
        if inverse is None:
            inverse = [eye - jnp.where(lower, a, 0.0) for a in among]
        else:
            halves = [split(x) for x in inverse]
            right = [
                split(dot3(split(jnp.where(lower, a, 0.0)), x)) for a, x in zip(among, halves)
            ]
            inverse = [x - dot3(h, r) for x, h, r in zip(inverse, halves, right)]
        size *= 2
    return inverse


def running(g):
    row, col = masks()
    cum = mm((row >= col).astype(BF), g)
    return cum, cum[L // 2 : L // 2 + 1, :], cum[L - 1 : L, :]


def compose(later, earlier):
    product = dot3(split(later[:, :DK]), split(earlier))
    return jnp.concatenate([product[:, :DK], product[:, DK:] + later[:, DK:]], 1)


def advance(span, state):
    return dot3(split(span[:, :DK]), split(state)) + span[:, DK:]


def kernel(
    q_ref, k_ref, v_ref, g_ref, rate_ref, out_ref,
    kb, gb, vb, qb, rb, ob, inv, past, behind, weight, spans,
    sib, chip, first, xb, before, yb, enter,
    in_send, in_recv, out_send, out_recv, rate_send, rate_recv, scan_send, scan_recv,
):
    me = lax.axis_index("seq")
    z = lax.axis_index("head")
    core, x, y = me % 2, (me // 2) % 4, me // 8
    peer = me + 1 - 2 * core
    x_peers = [y * 8 + ((x + d) % 4) * 2 + core for d in (1, 2, 3)]
    y_peers = [((y + d) % 4) * 8 + x * 2 + core for d in (1, 2, 3)]
    row, col = masks()
    eye = row == col

    barrier = pltpu.get_barrier_semaphore()

    def greet(d, carry):
        pl.semaphore_signal(barrier, inc=1, device_id=(me, (z + d) % RING), device_id_type=MESH)
        return carry

    lax.fori_loop(1, RING, greet, 0)
    for to in [peer] + x_peers + y_peers:
        pl.semaphore_signal(barrier, inc=1, device_id=(to, z), device_id_type=MESH)
    pl.semaphore_wait(barrier, RING + 6)

    def columns(owner, h):
        return pl.ds(pl.multiple_of((owner * HEADS + h) * DK, DK), DK)

    def remote(src, dst, send, recv, to):
        return pltpu.make_async_remote_copy(
            src_ref=src, dst_ref=dst, send_sem=send, recv_sem=recv, device_id=to, device_id_type=MESH
        )

    arrays = ((k_ref, kb), (g_ref, gb), (v_ref, vb), (q_ref, qb))

    def incoming(a, h, d):
        to = (z + d) % RING
        src, dst = arrays[a]
        return remote(
            src.at[:, columns(to, h)], dst.at[h, d], in_send.at[a, h, d], in_recv.at[a, h, d], (me, to)
        )

    def own_block(a, h):
        src, dst = arrays[a]
        return pltpu.make_async_copy(src.at[:, columns(z, h)], dst.at[h, 0], in_recv.at[a, h, 0])

    def rate_part(owner):
        return rate_ref.at[pl.ds(pl.multiple_of(owner // 4 * 16, 16), 16), :]

    def rates(d):
        to = (z + d) % RING
        return remote(rate_part(to), rb.at[d], rate_send.at[d], rate_recv.at[d], (me, to))

    def outgoing(h, d):
        to = (z + d) % RING
        return remote(
            ob.at[h, d], out_ref.at[:, columns(z, h)], out_send.at[h, d], out_recv.at[h, d], (me, to)
        )

    def own_out(h):
        return pltpu.make_async_copy(ob.at[h, 0], out_ref.at[:, columns(z, h)], out_recv.at[h, 0])

    own_rate = pltpu.make_async_copy(rate_part(z), rb.at[0], rate_recv.at[0])

    def over_peers(act):
        def one(d, carry):
            act(d)
            return carry

        lax.fori_loop(1, RING, one, 0)

    def start_in(which, h):
        for a in which:
            own_block(a, h).start()
            over_peers(lambda d: incoming(a, h, d).start())

    def wait_in(which, h):
        for a in which:
            own_block(a, h).wait()
            over_peers(lambda d: incoming(a, h, d).wait_recv())

    own_rate.start()
    over_peers(lambda d: rates(d).start())

    def send_three(h, carry):
        start_in((0, 1, 2), h)
        return carry

    def send_query(h, carry):
        start_in((3,), h)
        return carry

    lax.fori_loop(0, HEADS, send_three, 0)
    lax.fori_loop(0, HEADS, send_query, 0)
    own_rate.wait()
    over_peers(lambda d: rates(d).wait_recv())

    def maps(h):
        spans[h, 0] = jnp.concatenate([jnp.where(eye, 1.0, 0.0), jnp.zeros((L, DK), F32)], 1)
        mine = lax.broadcasted_iota(jnp.int32, rb.shape[1:], 0) == z % 4 * HEADS + h

        def group(n, carry):
            pre = []
            for i in range(RING):
                b = n * RING + i
                slot = (z - b + RING) % RING
                rate = jnp.sum(jnp.where(mine, rb[slot].astype(F32), 0.0), axis=0, keepdims=True)
                weight[h, b] = rate
                cum, mid, closing = running(gb[h, slot])
                kn = unit_rows(kb[h, slot].astype(F32))
                back = kn * jnp.exp(mid - cum)
                kp = kn * jnp.exp(cum)
                behind[h, b] = back
                past[h, b] = kp
                pre.append(
                    (
                        split(kn * jnp.exp(cum - mid)),
                        split(back),
                        split(kp),
                        split((kn * jnp.exp(closing - cum)).T * rate),
                        jnp.where(eye, jnp.exp(closing), 0.0),
                        vb[h, slot],
                        rate,
                    )
                )
            among = [jnp.where(row > col, dot3(p[0], p[1], True), 0.0) * p[6] for p in pre]
            inverse = unit_inverse(among)
            steps = []
            for i in range(RING):
                inv[h, n * RING + i] = inverse[i]
                reach = split(dot3(pre[i][3], split(inverse[i])))
                steps.append((pre[i][4] - dot3(reach, pre[i][2]), dot2(reach, pre[i][5])))
            prefix = spans[h, n * RING]
            for i in range(RING):
                prefix = compose(jnp.concatenate(steps[i], 1), prefix)
                spans[h, n * RING + i + 1] = prefix
            return carry

        group(0, 0)

    def read_out(h, state):
        halves = split(state)

        def group(n, carry):
            entry, update = [], []
            for i in range(GROUP):
                b = n * GROUP + i
                slot = (z - b + RING) % RING
                span = spans[h, b]
                s = dot3(split(span[:, :DK]), halves) + span[:, DK:]
                entry.append(s)
            for i in range(GROUP):
                b = n * GROUP + i
                slot = (z - b + RING) % RING
                rest = vb[h, slot].astype(F32) - dot3(split(past[h, b]), split(entry[i]))
                update.append(dot3(split(inv[h, b]), split(rest)))
            for i in range(GROUP):
                b = n * GROUP + i
                slot = (z - b + RING) % RING
                cum, mid, closing = running(gb[h, slot])
                qn = unit_rows(qb[h, slot].astype(F32))
                attend = dot3(split(qn * jnp.exp(cum - mid)), split(behind[h, b]), True)
                attend = jnp.where(row >= col, attend, 0.0) * weight[h, b]
                left = jnp.concatenate([qn * jnp.exp(cum), attend], 1)
                right = jnp.concatenate([entry[i], update[i]], 0)
                l, r = split(left), split(right)
                out = mm(l[0], r[0]) + (mm(l[0], r[1]) + mm(l[1], r[0]))
                ob[h, (b - z + RING) % RING] = out.astype(BF)
            for i in range(GROUP):
                d = (n * GROUP + i - z + RING) % RING
                pl.when(d == 0)(lambda: own_out(h).start())
                pl.when(d != 0)(lambda d=d: outgoing(h, d).start())
            return carry

        lax.fori_loop(0, RING // GROUP, group, 0)

    def to_sibling(j):
        return remote(
            spans.at[2 * j + 1 - core, RING], sib.at[j], scan_send.at[j, 0], scan_recv.at[j, 0], (peer, z)
        )

    def to_x(j, d):
        return remote(
            chip.at[j], xb.at[j, d], scan_send.at[j, 1 + d], scan_recv.at[j, 1 + d], (x_peers[d], z)
        )

    def to_y(j, d):
        return remote(
            yb.at[j, 3], yb.at[j, d], scan_send.at[j, 4 + d], scan_recv.at[j, 4 + d], (y_peers[d], z)
        )

    def on_y(j, start):
        for d in range(3):
            if start:
                pl.when(y + d + 1 < 4)(lambda d=d: to_y(j, d).start())
            else:
                pl.when(y >= d + 1)(lambda d=d: to_y(j, d).wait_recv())

    def to_enter(j):
        return remote(
            enter.at[j, 1], enter.at[j, 2], scan_send.at[j, 7], scan_recv.at[j, 7], (peer, z)
        )

    def over_chip(j):
        to_sibling(j).wait_recv()
        own, other = spans[2 * j + core, RING], sib[j]
        first[j] = jnp.where(core == 0, own, other)
        chip[j] = compose(jnp.where(core == 0, other, own), first[j])
        for d in range(3):
            to_x(j, d).start()

    def over_x(j):
        for d in range(3):
            to_x(j, d).wait_recv()
        place = []
        for i in range(4):
            far = (x - i + 4) % 4
            place.append(
                jnp.where(
                    far == 0,
                    chip[j],
                    jnp.where(far == 1, xb[j, 0], jnp.where(far == 2, xb[j, 1], xb[j, 2])),
                )
            )
        two = compose(place[1], place[0])
        yb[j, 3] = compose(compose(place[3], place[2]), two)
        on_y(j, True)
        three = compose(place[2], two)
        before[j] = jnp.where(
            x == 0,
            spans[0, 0],
            jnp.where(x == 1, place[0], jnp.where(x == 2, two, three)),
        )

    def over_y(j):
        on_y(j, False)
        place = []
        for i in range(3):
            far = (y - i + 4) % 4
            place.append(
                jnp.where(
                    far == 0,
                    yb[j, 3],
                    jnp.where(far == 1, yb[j, 0], jnp.where(far == 2, yb[j, 1], yb[j, 2])),
                )
            )
        one = place[0][:, DK:]
        two = advance(place[1], one)
        three = advance(place[2], two)
        state = jnp.where(y == 0, 0.0, jnp.where(y == 1, one, jnp.where(y == 2, two, three)))
        state = advance(before[j], state)
        after = advance(first[j], state)
        enter[j, 0] = jnp.where(core == 0, state, after)
        enter[j, 1] = jnp.where(core == 0, after, state)
        to_enter(j).start()

    def turn_in(h, carry):
        pl.when(h == 2)(lambda: over_chip(0))
        wait_in((0, 1, 2), h)
        maps(h)
        pl.when(h == 1)(lambda: to_sibling(0).start())
        pl.when(h == 2)(lambda: over_x(0))
        pl.when(h == 3)(lambda: to_sibling(1).start())
        return carry

    lax.fori_loop(0, HEADS, turn_in, 0)

    def turn_out(h, carry):
        @pl.when(h == 0)
        def _():
            over_y(0)
            over_chip(1)
            to_enter(0).wait_recv()

        pl.when(h == 1)(lambda: over_x(1))

        @pl.when(h == 2)
        def _():
            over_y(1)
            to_enter(1).wait_recv()

        wait_in((3,), h)
        j, half = h // 2, h % 2
        read_out(h, jnp.where(core == half, enter[j, 0], enter[j, 2]))
        return carry

    lax.fori_loop(0, HEADS, turn_out, 0)

    def sent(h, carry):
        for a in range(4):
            over_peers(lambda d: incoming(a, h, d).wait_send())
        return carry

    lax.fori_loop(0, HEADS, sent, 0)
    over_peers(lambda d: rates(d).wait_send())
    for j in range(2):
        to_sibling(j).wait_send()
        to_enter(j).wait_send()
        for d in range(3):
            to_x(j, d).wait_send()
            pl.when(y + d + 1 < 4)(lambda d=d: to_y(j, d).wait_send())

    def finish(h, carry):
        own_out(h).wait()
        over_peers(lambda d: outgoing(h, d).wait())
        return carry

    lax.fori_loop(0, HEADS, finish, 0)


def local(query_rows, key_rows, value_rows, log_decay, write_rate):
    rows = write_rate.shape[0]
    anywhere = pl.BlockSpec(memory_space=pltpu.HBM)
    block = pltpu.VMEM((HEADS, RING, L, DK), BF)
    wide = pltpu.VMEM((HEADS, RING, L, DK), F32)
    pair = pltpu.VMEM((2, DK, 2 * DK), F32)
    return pl.pallas_call(
        kernel,
        in_specs=[anywhere] * 5,
        out_specs=pl.BlockSpec(memory_space=pltpu.VMEM),
        out_shape=jax.ShapeDtypeStruct(query_rows.shape, BF),
        scratch_shapes=[
            block,
            block,
            block,
            block,
            pltpu.VMEM((RING, 16, rows), BF),
            block,
            wide,
            wide,
            wide,
            pltpu.VMEM((HEADS, RING, 1, L), F32),
            pltpu.VMEM((HEADS, RING + 1, DK, 2 * DK), F32),
            pair,
            pair,
            pair,
            pltpu.VMEM((2, 3, DK, 2 * DK), F32),
            pair,
            pltpu.VMEM((2, 4, DK, 2 * DK), F32),
            pltpu.VMEM((2, 3, DK, DK), F32),
            pltpu.SemaphoreType.DMA((4, HEADS, RING)),
            pltpu.SemaphoreType.DMA((4, HEADS, RING)),
            pltpu.SemaphoreType.DMA((HEADS, RING)),
            pltpu.SemaphoreType.DMA((HEADS, RING)),
            pltpu.SemaphoreType.DMA((RING,)),
            pltpu.SemaphoreType.DMA((RING,)),
            pltpu.SemaphoreType.DMA((2, 8)),
            pltpu.SemaphoreType.DMA((2, 8)),
        ],
        compiler_params=pltpu.CompilerParams(
            vmem_limit_bytes=LIMIT * 2**20, collective_id=0, has_side_effects=True
        ),
    )(query_rows, key_rows, value_rows, log_decay, write_rate.T)


def solution(mesh):
    spec = P(("seq", "head"), None)
    return jax.shard_map(
        local, mesh=mesh, in_specs=(spec,) * 5, out_specs=spec, check_vma=False
    )
```

```python
import functools

import jax
import jax.numpy as jnp
from jax import lax
from jax.experimental import pallas as pl
from jax.experimental.pallas import tpu as pltpu
from jax.sharding import PartitionSpec as P

DK = 128
L = 128
RING = 8
LIMIT = 52
HEADS = 4
GROUP = 4
F32 = jnp.float32
BF = jnp.bfloat16
MESH = pl.DeviceIdType.MESH


def split(x):
    hi = x.astype(BF)
    return hi, (x - hi.astype(F32)).astype(BF)


def mm(a, b, dims=((1,), (0,))):
    return lax.dot_general(a, b, (dims, ((), ())), preferred_element_type=F32)


def dot3(a, b, turned=False):
    wide = jnp.concatenate([a[0], a[1]], 1)
    if turned:
        both = jnp.concatenate([b[0], b[1]], 0)
        product = mm(wide, jnp.concatenate([both, both], 1), ((1,), (1,)))
    else:
        both = jnp.concatenate([b[0], b[1]], 1)
        product = mm(wide, jnp.concatenate([both, both], 0))
    half = product.shape[1] // 2
    return product[:, :half] + product[:, half:]


def dot2(a, b):
    return mm(jnp.concatenate([a[0], a[1]], 1), jnp.concatenate([b, b], 0))


def unit_rows(x):
    return x * lax.rsqrt(jnp.sum(x * x, axis=-1, keepdims=True) + 1e-6)


def masks():
    row = lax.broadcasted_iota(jnp.int32, (L, L), 0)
    col = lax.broadcasted_iota(jnp.int32, (L, L), 1)
    return row, col


def unit_inverse(among):
    row, col = masks()
    eye = jnp.where(row == col, 1.0, 0.0)
    inverse = None
    size = 1
    while size < L:
        lower = jnp.logical_and(
            row // (2 * size) == col // (2 * size),
            jnp.logical_and((row // size) % 2 == 1, (col // size) % 2 == 0),
        )
        if inverse is None:
            inverse = [eye - jnp.where(lower, a, 0.0) for a in among]
        else:
            halves = [split(x) for x in inverse]
            right = [
                split(dot3(split(jnp.where(lower, a, 0.0)), x)) for a, x in zip(among, halves)
            ]
            inverse = [x - dot3(h, r) for x, h, r in zip(inverse, halves, right)]
        size *= 2
    return inverse


def running(g):
    row, col = masks()
    cum = mm((row >= col).astype(BF), g)
    return cum, cum[L // 2 : L // 2 + 1, :], cum[L - 1 : L, :]


def compose(later, earlier):
    product = dot3(split(later[:, :DK]), split(earlier))
    return jnp.concatenate([product[:, :DK], product[:, DK:] + later[:, DK:]], 1)


def advance(span, state):
    return dot3(split(span[:, :DK]), split(state)) + span[:, DK:]


def kernel(
    q_ref, k_ref, v_ref, g_ref, rate_ref, out_ref,
    kb, gb, vb, qb, rb, ob, inv, past, behind, weight, spans,
    sib, chip, first, xb, before, yb, enter,
    in_send, in_recv, out_send, out_recv, rate_send, rate_recv, scan_send, scan_recv,
):
    me = lax.axis_index("seq")
    z = lax.axis_index("head")
    core, x, y = me % 2, (me // 2) % 4, me // 8
    peer = me + 1 - 2 * core
    x_peers = [y * 8 + ((x + d) % 4) * 2 + core for d in (1, 2, 3)]
    y_peers = [((y + d) % 4) * 8 + x * 2 + core for d in (1, 2, 3)]
    row, col = masks()
    eye = row == col

    def columns(owner, h):
        return pl.ds(pl.multiple_of((owner * HEADS + h) * DK, DK), DK)

    def remote(src, dst, send, recv, to):
        return pltpu.make_async_remote_copy(
            src_ref=src, dst_ref=dst, send_sem=send, recv_sem=recv, device_id=to, device_id_type=MESH
        )

    arrays = ((k_ref, kb), (g_ref, gb), (v_ref, vb), (q_ref, qb))

    def incoming(a, h, d):
        to = (z + d) % RING
        src, dst = arrays[a]
        return remote(
            src.at[:, columns(to, h)], dst.at[h, d], in_send.at[a, h, d], in_recv.at[a, h, d], (me, to)
        )

    def own_block(a, h):
        src, dst = arrays[a]
        return pltpu.make_async_copy(src.at[:, columns(z, h)], dst.at[h, 0], in_recv.at[a, h, 0])

    def rate_part(owner):
        return rate_ref.at[pl.ds(pl.multiple_of(owner // 4 * 16, 16), 16), :]

    def rates(d):
        to = (z + d) % RING
        return remote(rate_part(to), rb.at[d], rate_send.at[d], rate_recv.at[d], (me, to))

    def outgoing(h, d):
        to = (z + d) % RING
        return remote(
            ob.at[h, d], out_ref.at[:, columns(z, h)], out_send.at[h, d], out_recv.at[h, d], (me, to)
        )

    def own_out(h):
        return pltpu.make_async_copy(ob.at[h, 0], out_ref.at[:, columns(z, h)], out_recv.at[h, 0])

    own_rate = pltpu.make_async_copy(rate_part(z), rb.at[0], rate_recv.at[0])

    def over_peers(act):
        def one(d, carry):
            act(d)
            return carry

        lax.fori_loop(1, RING, one, 0)

    def start_in(which, h):
        for a in which:
            over_peers(lambda d: incoming(a, h, d).start())

    def wait_in(which, h):
        for a in which:
            own_block(a, h).wait()
            over_peers(lambda d: incoming(a, h, d).wait_recv())


    def send_three(h, carry):
        start_in((0, 1, 2), h)
        return carry

    def send_query(h, carry):
        start_in((3,), h)
        return carry

    own_rate.start()

    def keep_own(h, carry):
        for a in range(4):
            own_block(a, h).start()
        return carry

    barrier = pltpu.get_barrier_semaphore()

    def greet(d, carry):
        pl.semaphore_signal(barrier, inc=1, device_id=(me, (z + d) % RING), device_id_type=MESH)
        return carry

    for to in [peer] + x_peers + y_peers:
        pl.semaphore_signal(barrier, inc=1, device_id=(to, z), device_id_type=MESH)
    lax.fori_loop(1, RING, greet, 0)
    lax.fori_loop(0, HEADS, keep_own, 0)
    pl.semaphore_wait(barrier, RING + 6)

    send_three(0, 0)
    over_peers(lambda d: rates(d).start())
    lax.fori_loop(1, HEADS, send_three, 0)
    lax.fori_loop(0, HEADS, send_query, 0)
    own_rate.wait()
    over_peers(lambda d: rates(d).wait_recv())

    def maps(h):
        spans[h, 0] = jnp.concatenate([jnp.where(eye, 1.0, 0.0), jnp.zeros((L, DK), F32)], 1)
        mine = lax.broadcasted_iota(jnp.int32, rb.shape[1:], 0) == z % 4 * HEADS + h

        def group(n, carry):
            pre = []
            for i in range(RING):
                b = n * RING + i
                slot = (z - b + RING) % RING
                rate = jnp.sum(jnp.where(mine, rb[slot].astype(F32), 0.0), axis=0, keepdims=True)
                weight[h, b] = rate
                cum, mid, closing = running(gb[h, slot])
                kn = unit_rows(kb[h, slot].astype(F32))
                back = kn * jnp.exp(mid - cum)
                kp = kn * jnp.exp(cum)
                behind[h, b] = back
                past[h, b] = kp
                pre.append(
                    (
                        split(kn * jnp.exp(cum - mid)),
                        split(back),
                        split(kp),
                        split((kn * jnp.exp(closing - cum)).T * rate),
                        jnp.where(eye, jnp.exp(closing), 0.0),
                        vb[h, slot],
                        rate,
                    )
                )
            among = [jnp.where(row > col, dot3(p[0], p[1], True), 0.0) * p[6] for p in pre]
            inverse = unit_inverse(among)
            steps = []
            for i in range(RING):
                inv[h, n * RING + i] = inverse[i]
                reach = split(dot3(pre[i][3], split(inverse[i])))
                steps.append((pre[i][4] - dot3(reach, pre[i][2]), dot2(reach, pre[i][5])))
            prefix = spans[h, n * RING]
            for i in range(RING):
                prefix = compose(jnp.concatenate(steps[i], 1), prefix)
                spans[h, n * RING + i + 1] = prefix
            return carry

        group(0, 0)

    def read_out(h, state):
        halves = split(state)

        def group(n, carry):
            entry, update = [], []
            for i in range(GROUP):
                b = n * GROUP + i
                slot = (z - b + RING) % RING
                span = spans[h, b]
                s = dot3(split(span[:, :DK]), halves) + span[:, DK:]
                entry.append(s)
            for i in range(GROUP):
                b = n * GROUP + i
                slot = (z - b + RING) % RING
                rest = vb[h, slot].astype(F32) - dot3(split(past[h, b]), split(entry[i]))
                update.append(dot3(split(inv[h, b]), split(rest)))
            for i in range(GROUP):
                b = n * GROUP + i
                slot = (z - b + RING) % RING
                cum, mid, closing = running(gb[h, slot])
                qn = unit_rows(qb[h, slot].astype(F32))
                attend = dot3(split(qn * jnp.exp(cum - mid)), split(behind[h, b]), True)
                attend = jnp.where(row >= col, attend, 0.0) * weight[h, b]
                left = jnp.concatenate([qn * jnp.exp(cum), attend], 1)
                right = jnp.concatenate([entry[i], update[i]], 0)
                l, r = split(left), split(right)
                out = mm(l[0], r[0]) + (mm(l[0], r[1]) + mm(l[1], r[0]))
                ob[h, (b - z + RING) % RING] = out.astype(BF)
            for i in range(GROUP):
                d = (n * GROUP + i - z + RING) % RING
                pl.when(d == 0)(lambda: own_out(h).start())
                pl.when(d != 0)(lambda d=d: outgoing(h, d).start())
            return carry

        lax.fori_loop(0, RING // GROUP, group, 0)

    def to_sibling(j):
        return remote(
            spans.at[2 * j + 1 - core, RING], sib.at[j], scan_send.at[j, 0], scan_recv.at[j, 0], (peer, z)
        )

    def to_x(j, d):
        return remote(
            chip.at[j], xb.at[j, d], scan_send.at[j, 1 + d], scan_recv.at[j, 1 + d], (x_peers[d], z)
        )

    def to_y(j, d):
        return remote(
            yb.at[j, 3], yb.at[j, d], scan_send.at[j, 4 + d], scan_recv.at[j, 4 + d], (y_peers[d], z)
        )

    def on_y(j, start):
        for d in range(3):
            if start:
                pl.when(y + d + 1 < 4)(lambda d=d: to_y(j, d).start())
            else:
                pl.when(y >= d + 1)(lambda d=d: to_y(j, d).wait_recv())

    def to_enter(j):
        return remote(
            enter.at[j, 1], enter.at[j, 2], scan_send.at[j, 7], scan_recv.at[j, 7], (peer, z)
        )

    def over_chip(j):
        to_sibling(j).wait_recv()
        own, other = spans[2 * j + core, RING], sib[j]
        first[j] = jnp.where(core == 0, own, other)
        chip[j] = compose(jnp.where(core == 0, other, own), first[j])
        for d in range(3):
            to_x(j, d).start()

    def over_x(j):
        for d in range(3):
            to_x(j, d).wait_recv()
        place = []
        for i in range(4):
            far = (x - i + 4) % 4
            place.append(
                jnp.where(
                    far == 0,
                    chip[j],
                    jnp.where(far == 1, xb[j, 0], jnp.where(far == 2, xb[j, 1], xb[j, 2])),
                )
            )
        two = compose(place[1], place[0])
        yb[j, 3] = compose(compose(place[3], place[2]), two)
        on_y(j, True)
        three = compose(place[2], two)
        before[j] = jnp.where(
            x == 0,
            spans[0, 0],
            jnp.where(x == 1, place[0], jnp.where(x == 2, two, three)),
        )

    def over_y(j):
        on_y(j, False)
        place = []
        for i in range(3):
            far = (y - i + 4) % 4
            place.append(
                jnp.where(
                    far == 0,
                    yb[j, 3],
                    jnp.where(far == 1, yb[j, 0], jnp.where(far == 2, yb[j, 1], yb[j, 2])),
                )
            )
        one = place[0][:, DK:]
        two = advance(place[1], one)
        three = advance(place[2], two)
        state = jnp.where(y == 0, 0.0, jnp.where(y == 1, one, jnp.where(y == 2, two, three)))
        state = advance(before[j], state)
        after = advance(first[j], state)
        enter[j, 0] = jnp.where(core == 0, state, after)
        enter[j, 1] = jnp.where(core == 0, after, state)
        to_enter(j).start()

    def turn_in(h, carry):
        pl.when(h == 2)(lambda: over_chip(0))
        wait_in((0, 1, 2), h)
        maps(h)
        pl.when(h == 1)(lambda: to_sibling(0).start())
        pl.when(h == 2)(lambda: over_x(0))
        pl.when(h == 3)(lambda: to_sibling(1).start())
        return carry

    lax.fori_loop(0, HEADS, turn_in, 0)

    def turn_out(h, carry):
        @pl.when(h == 0)
        def _():
            over_y(0)
            over_chip(1)
            to_enter(0).wait_recv()

        pl.when(h == 1)(lambda: over_x(1))

        @pl.when(h == 2)
        def _():
            over_y(1)
            to_enter(1).wait_recv()

        wait_in((3,), h)
        j, half = h // 2, h % 2
        read_out(h, jnp.where(core == half, enter[j, 0], enter[j, 2]))
        return carry

    lax.fori_loop(0, HEADS, turn_out, 0)

    def sent(h, carry):
        for a in range(4):
            over_peers(lambda d: incoming(a, h, d).wait_send())
        return carry

    lax.fori_loop(0, HEADS, sent, 0)
    over_peers(lambda d: rates(d).wait_send())
    for j in range(2):
        to_sibling(j).wait_send()
        to_enter(j).wait_send()
        for d in range(3):
            to_x(j, d).wait_send()
            pl.when(y + d + 1 < 4)(lambda d=d: to_y(j, d).wait_send())

    def finish(h, carry):
        own_out(h).wait()
        over_peers(lambda d: outgoing(h, d).wait())
        return carry

    lax.fori_loop(0, HEADS, finish, 0)


def local(query_rows, key_rows, value_rows, log_decay, write_rate):
    rows = write_rate.shape[0]
    anywhere = pl.BlockSpec(memory_space=pltpu.HBM)
    block = pltpu.VMEM((HEADS, RING, L, DK), BF)
    wide = pltpu.VMEM((HEADS, RING, L, DK), F32)
    pair = pltpu.VMEM((2, DK, 2 * DK), F32)
    return pl.pallas_call(
        kernel,
        in_specs=[anywhere] * 5,
        out_specs=pl.BlockSpec(memory_space=pltpu.VMEM),
        out_shape=jax.ShapeDtypeStruct(query_rows.shape, BF),
        scratch_shapes=[
            block,
            block,
            block,
            block,
            pltpu.VMEM((RING, 16, rows), BF),
            block,
            wide,
            wide,
            wide,
            pltpu.VMEM((HEADS, RING, 1, L), F32),
            pltpu.VMEM((HEADS, RING + 1, DK, 2 * DK), F32),
            pair,
            pair,
            pair,
            pltpu.VMEM((2, 3, DK, 2 * DK), F32),
            pair,
            pltpu.VMEM((2, 4, DK, 2 * DK), F32),
            pltpu.VMEM((2, 3, DK, DK), F32),
            pltpu.SemaphoreType.DMA((4, HEADS, RING)),
            pltpu.SemaphoreType.DMA((4, HEADS, RING)),
            pltpu.SemaphoreType.DMA((HEADS, RING)),
            pltpu.SemaphoreType.DMA((HEADS, RING)),
            pltpu.SemaphoreType.DMA((RING,)),
            pltpu.SemaphoreType.DMA((RING,)),
            pltpu.SemaphoreType.DMA((2, 8)),
            pltpu.SemaphoreType.DMA((2, 8)),
        ],
        compiler_params=pltpu.CompilerParams(
            vmem_limit_bytes=LIMIT * 2**20, collective_id=0, has_side_effects=True
        ),
    )(query_rows, key_rows, value_rows, log_decay, write_rate.T)


def solution(mesh):
    spec = P(("seq", "head"), None)
    return jax.shard_map(
        local, mesh=mesh, in_specs=(spec,) * 5, out_specs=spec, check_vma=False
    )
```
